32 devices in a mesh: tile: 8 (over y, x, core), vis: 4 (over z).
Axes of the slice: x: 2, y: 2, z: 4, core: 2. Of those that a mesh axis runs over, the one named last changes fastest.
Arguments:
- pieces: float32 [1024, 16, 1024], P(('tile', 'vis')), may hold values from -6 to 6
- coeffs: float32 [1024, 5, 4], P(('tile', 'vis')), may hold values from -1.8 to 1.8
- weights: float32 [1024], P(('tile', 'vis')), may hold values from 0.1 to 1
- routes: int32 [1024, 1], P(('tile', 'vis')), may hold values from 0 to 7; in each aligned block of 32 rows (0 to 31, 32 to 63, ...) at most 8 rows name the same one
- offsets: int32 [1024], P(('tile', 'vis')), may hold values from 0 to 63
Outputs:
- coadd: float32 [8192, 1024], P(('tile', 'vis'))
- detection: float32 [8192, 1024], P(('tile', 'vis'))
The draws below stay inside these ranges and needn't reach their ends.
Inputs may be any that keep to these rules, and one draw needn't show every extreme that they name: `routes`: among the 32 pieces of one device no strip index appears more than 8 times, and some index appears exactly 8 times; every strip index appears somewhere.
All inputs are finite; a program needn't handle non-finite values.
Results may differ from the reference program's by a relative error of at most 0.0003.
Values sent between devices are 32-bit elements; how exact they have to be, the bound alone decides.
A program may use at most 128 MiB of HBM per device.

```python
import math
import jax
import jax.numpy as jnp
import numpy as np
from jax import lax

SC = 1024
PR = 16
PIECES_DEV = 32
NROW = 5
NCOL = 4
TAPS = 10
REACH = 15
CAP = 8
NBLK = 64
PIECES = 1024
TRACT_ROWS = 8192
N_TILE = 8


def place_ends(values, rng, least, largest):
    extent = values.shape
    place = [jax.random.randint(jax.random.fold_in(rng, axis), (), 0, extent[axis]) for axis in range(len(extent))]
    values = values.at[tuple(place)].set(least)
    longest = extent.index(max(extent))
    place[longest] = (place[longest] + 1) % extent[longest]
    return values.at[tuple(place)].set(largest)


def block_levels(rng, shape, cuts, least, top_value):
    def one(dim, parts):
        heights = jax.random.uniform(jax.random.fold_in(jax.random.fold_in(rng, 6), dim), (parts,), jnp.float32, least / len(cuts), top_value / len(cuts))
        return jnp.repeat(jnp.exp(heights), shape[dim] // parts).reshape((-1,) + (1,) * (len(shape) - dim - 1))

    factor_of = one(*cuts[0])
    for cut in cuts[1:]:
        factor_of = factor_of * one(*cut)
    return factor_of


def shared_out(rng, own, number, rows, count, top, limit, lean):
    order = jax.random.permutation(rng, count)
    crowded, ordinary = load_shares(count, rows * top, limit, lean, True), load_shares(count, rows * top, limit, lean, False)
    places = jnp.arange(count)

    def named(sizes, offset_by):
        used = int((sizes > 0).sum())
        fixed = max(1, used // 4)
        passed = fixed + (places - fixed + offset_by * (used - fixed)) % max(1, count - fixed)
        return jnp.zeros((count,), jnp.int32).at[order[jnp.where(places < fixed, places, passed)]].set(jnp.asarray(sizes, jnp.int32))

    sizes = jnp.where(number % 4 == 0, named(crowded, number // 4), named(ordinary, number - number // 4 - 1))
    mixed = jax.random.permutation(jax.random.fold_in(own, 3), count)
    donor, taker = mixed[0:count // 2 * 2:2], mixed[1:count // 2 * 2:2]
    margin = jnp.minimum(sizes[donor] - 1, limit - sizes[taker]) // 2
    margin = jnp.where((donor == order[0]) | (taker == order[0]) | (sizes[taker] == 0), 0, jnp.maximum(margin, 0))
    passed = jax.random.randint(jax.random.fold_in(own, 4), (count // 2,), 0, 1 << 20) % (margin + 1)
    sizes = sizes.at[donor].add(-passed).at[taker].add(passed)
    labels = jnp.searchsorted(jnp.cumsum(sizes), jnp.arange(rows * top), side="right").astype(jnp.int32)
    listing = labels.reshape(top, rows).T
    listing = listing[jax.random.permutation(jax.random.fold_in(own, 1), rows)]
    offset_by = jax.random.randint(jax.random.fold_in(own, 2), (rows, 1), 0, top)
    return jnp.take_along_axis(listing, (jnp.arange(top)[None, :] + offset_by) % top, axis=1)


def load_shares(count, total, most, lean, full):
    weights = [(1 << 20) // math.isqrt(rank ** lean) + 1 for rank in range(1, count + 1)]
    largest = most if full else min(most, max(-(-total // count), total * weights[0] // sum(weights)))
    least = 1 if total - largest >= count - 1 else 0
    counts, spare = [largest] + [least] * (count - 1), total - largest - least * (count - 1)
    while spare > 0:
        free = [i for i in range(1, count) if counts[i] < largest] or [i for i in range(1, count) if counts[i] < most]
        mass, remaining = sum([weights[i] for i in free]), spare
        for i in free:
            addition = min(most - counts[i], max(1, remaining * weights[i] // mass), spare)
            counts[i] = counts[i] + addition
            spare = spare - addition
    return np.array(counts)


def normal_values(own_key, dims, deviation, reach, cuts=(), dtype=jnp.bfloat16):
    loudness = block_levels(own_key, dims, cuts, -0.22, 0.18) if cuts else 1.0
    values = jax.random.normal(own_key, dims, jnp.float32) * deviation * loudness
    return jnp.minimum(jnp.maximum(values, -reach), reach).astype(dtype)


def setup_inputs(seed: int = 0) -> dict:
    seeds = jax.random.split(jax.random.key(seed), 6)
    pieces = normal_values(seeds[0], (PIECES, PR, SC), 1.0, 6.0, ((0, 32),), jnp.float32)
    coeffs = normal_values(seeds[1], (PIECES, NROW, NCOL), 0.3, 1.8, ((0, 32),), jnp.float32)
    weights = jnp.clip(jnp.exp(math.log(1.0) - 2.3025851 * jax.random.uniform(seeds[2], (PIECES,), jnp.float32) ** block_levels(seeds[2], (PIECES,), ((0, 32),), -0.2, 0.2)), 0.1, 1.0)
    routes_keys = jax.random.split(jax.random.fold_in(seeds[3], 1), PIECES // PIECES_DEV)
    routes_turns = jax.random.permutation(jax.random.fold_in(seeds[3], 3), PIECES // PIECES_DEV)
    routes = jax.vmap(lambda own, number: shared_out(jax.random.fold_in(seeds[3], 2), own, number, PIECES_DEV, N_TILE, 1, CAP, 2))(routes_keys, routes_turns).reshape((PIECES, 1))
    offsets = place_ends(jax.random.randint(seeds[4], (PIECES,), 0, NBLK), jax.random.fold_in(seeds[4], 1), 0, NBLK - 1).astype(jnp.int32)
    return {"pieces": pieces, "coeffs": coeffs, "weights": weights, "routes": routes, "offsets": offsets}


row_shapes = ((1.0, 0), (1.0, 1), (2.0, 0), (2.0, 2), (3.5, 0))
column_shapes = ((1.0, 0), (2.0, 0), (2.0, 1), (3.5, 0))
highest = lax.Precision.HIGHEST

def shaped_taps(lag_table, shape_list, tap_reach):
    tap_spots = jnp.arange(-tap_reach, tap_reach + 1).astype(jnp.float32)
    lagged = lag_table.astype(jnp.float32)
    stacked = []
    for spread, degree in shape_list:
        full_taps = jnp.exp(-tap_spots * tap_spots / (2.0 * spread * spread)) * (tap_spots / spread) ** degree
        unit_scale = 1.0 / jnp.sqrt(jnp.sum(full_taps * full_taps))
        values = jnp.exp(-lagged * lagged / (2.0 * spread * spread)) * (lagged / spread) ** degree * unit_scale
        stacked.append(jnp.where(jnp.abs(lag_table) <= tap_reach, values, 0.0))
    return jnp.stack(stacked)

def detect_taps(lag_table, tap_reach):
    tap_spots = jnp.arange(-tap_reach, tap_reach + 1).astype(jnp.float32)
    gauss_total = jnp.sum(jnp.exp(-tap_spots * tap_spots / 18.0))
    lagged = lag_table.astype(jnp.float32)
    values = jnp.exp(-lagged * lagged / 18.0) / gauss_total - 1.0 / (2 * tap_reach + 1)
    return jnp.where(jnp.abs(lag_table) <= tap_reach, values, 0.0)

def basis_tables(piece_rows):
    row_lag = jnp.arange(piece_rows)[None, :] - jnp.arange(piece_rows)[:, None]
    row_bank = shaped_taps(row_lag, row_shapes, TAPS)
    column_lag = jnp.arange(384)[:, None] - 128 - jnp.arange(128)[None, :]
    column_windows = shaped_taps(column_lag, column_shapes, TAPS)
    detect_windows = detect_taps(column_lag, REACH)[None]
    return (row_bank, column_windows, detect_windows)

def column_pass(images, windows):
    lead_count, kernel_count, rows_count, strip_width = images.shape
    blocks = strip_width // 128
    padded = jnp.pad(images, ((0, 0), (0, 0), (0, 0), (128, 128)))
    viewed = padded.reshape(lead_count, kernel_count, rows_count, blocks + 2, 128)
    framed = jnp.concatenate([viewed[:, :, :, 0:blocks], viewed[:, :, :, 1:blocks + 1], viewed[:, :, :, 2:blocks + 2]], axis=4)
    result = jnp.einsum('mnrjk,nko->mrjo', framed, windows, precision=highest)
    return result.reshape(lead_count, rows_count, strip_width)

def match_pieces(images, factors, row_bank, column_windows):
    rowed = jnp.einsum('aqp,mpc->maqc', row_bank, images, precision=highest)
    mixed = jnp.einsum('mab,maqc->mbqc', factors, rowed, precision=highest)
    return column_pass(mixed, column_windows)

def reference(pieces, coeffs, weights, routes, offsets):
    piece_rows = pieces.shape[1]
    strip_width = pieces.shape[2]
    row_bank, column_windows, detect_windows = basis_tables(piece_rows)
    batch_size = PIECES_DEV
    groups = pieces.shape[0] // batch_size
    segments_all = N_TILE * NBLK

    def one_group(running, group_data):
        numerator, weight_total = running
        images, factors, masses, targets, places = group_data
        matched = match_pieces(images, factors, row_bank, column_windows)
        segment = (targets[:, 0] * NBLK + places).astype(jnp.int32)
        numerator = numerator + jax.ops.segment_sum(matched * masses[:, None, None], segment, num_segments=segments_all)
        weight_total = weight_total + jax.ops.segment_sum(masses, segment, num_segments=segments_all)
        return ((numerator, weight_total), None)
    start_state = (jnp.zeros((segments_all, piece_rows, strip_width), jnp.float32), jnp.zeros((segments_all,), jnp.float32))
    grouped = (pieces.reshape(groups, batch_size, piece_rows, strip_width), coeffs.reshape(groups, batch_size, NROW, NCOL), weights.reshape(groups, batch_size), routes.reshape(groups, batch_size, 1), offsets.reshape(groups, batch_size))
    (numerator, weight_total), unused = lax.scan(one_group, start_state, grouped)
    has_weight = weight_total > 0.0
    divisor = jnp.where(has_weight, weight_total, 1.0)
    coadd = jnp.where(has_weight[:, None, None], numerator / divisor[:, None, None], 0.0).reshape(TRACT_ROWS, strip_width)
    filtered = column_pass(coadd[None, None], detect_windows)[0]
    padded = jnp.pad(filtered, ((REACH, REACH), (0, 0)))
    row_taps = detect_taps(jnp.arange(-REACH, REACH + 1), REACH)
    detection = jnp.zeros_like(filtered)
    for shift_index in range(2 * REACH + 1):
        detection = detection + row_taps[shift_index] * padded[shift_index:shift_index + TRACT_ROWS]
    return (coadd, detection)
```

```python
import functools

import jax
import jax.numpy as jnp
import ml_dtypes
import numpy as np
from jax import lax
from jax.experimental import pallas as pl
from jax.experimental.pallas import tpu as pltpu
from jax.sharding import PartitionSpec as P

SR = 1024
TAPS = 10
REACH = 15
LANES = 128
SIDE = 64
RIM = 16
GROUP = 4

row_shapes = ((1.0, 0), (1.0, 1), (2.0, 0), (2.0, 2), (3.5, 0))
column_shapes = ((1.0, 0), (2.0, 0), (2.0, 1), (3.5, 0))
highest = lax.Precision.HIGHEST
F32 = jnp.float32
BF16 = jnp.bfloat16


def shaped_taps(lags, shapes, reach):
    spots = np.arange(-reach, reach + 1).astype(np.float64)
    lags = lags.astype(np.float64)
    stacked = []
    for spread, degree in shapes:
        full = np.exp(-spots * spots / (2.0 * spread * spread)) * (spots / spread) ** degree
        values = np.exp(-lags * lags / (2.0 * spread * spread)) * (lags / spread) ** degree
        values = values / np.sqrt(np.sum(full * full))
        stacked.append(np.where(np.abs(lags) <= reach, values, 0.0))
    return np.stack(stacked)


def detect_taps(lags, reach):
    spots = np.arange(-reach, reach + 1).astype(np.float64)
    total = np.sum(np.exp(-spots * spots / 18.0))
    lags = lags.astype(np.float64)
    values = np.exp(-lags * lags / 18.0) / total - 1.0 / (2 * reach + 1)
    return np.where(np.abs(lags) <= reach, values, 0.0)


def halves_np(table):
    table = table.astype(np.float32)
    top = table.astype(ml_dtypes.bfloat16)
    rest = (table - top.astype(np.float32)).astype(ml_dtypes.bfloat16)
    return jnp.asarray(top), jnp.asarray(rest)


def halves(x):
    top = x.astype(BF16)
    return top, (x - top.astype(F32)).astype(BF16)


def dot(a, b):
    return jnp.dot(a, b, preferred_element_type=F32)


def window_lags():
    return np.arange(2 * SIDE + LANES)[:, None] - SIDE - np.arange(LANES)[None, :]


def windows_of(x):
    rows, width = x.shape
    rim = jnp.zeros((rows, SIDE), x.dtype)
    padded = jnp.concatenate([rim, x, rim], axis=1)
    blocks = width // LANES
    return jnp.concatenate(
        [padded[:, LANES * j : LANES * (j + 2)] for j in range(blocks)], axis=0
    )


def match_body(capacity, routes_ref, pieces_ref, mix_ref, top_ref, rest_ref, out_ref, count_ref):
    step = pl.program_id(0)
    pieces, rows, width = pieces_ref.shape
    kinds = top_ref.shape[1] // LANES
    blocks = width // LANES

    @pl.when(step == 0)
    def _():
        out_ref[...] = jnp.zeros_like(out_ref)

        @pl.loop(0, count_ref.shape[0])
        def _(i):
            count_ref[i] = 0

    flat = pieces_ref[...].reshape(pieces * rows, width)
    wide = windows_of(flat)
    top, rest = halves(wide)
    swept = dot(top, top_ref[...]) + (dot(rest, top_ref[...]) + dot(top, rest_ref[...]))
    span = GROUP * rows
    for q in range(pieces // GROUP):
        parts = []
        for j in range(blocks):
            at = j * pieces * rows + q * span
            parts.append(
                jnp.concatenate(
                    [swept[at : at + span, LANES * b : LANES * (b + 1)] for b in range(kinds)],
                    axis=0,
                )
            )
        banked = jnp.concatenate(parts, axis=1)
        y_top, y_rest = halves(banked)
        m_top, m_rest = halves(mix_ref[q])
        result = dot(m_top, y_top) + (dot(m_rest, y_top) + dot(m_top, y_rest))
        for i in range(GROUP):
            strip = routes_ref[step * pieces + q * GROUP + i]
            rank = count_ref[strip]
            count_ref[strip] = rank + 1
            out_ref[strip * capacity + rank] = result[i * rows : (i + 1) * rows]


def match(pieces, mix, routes, tiles, capacity):
    count, rows, width = pieces.shape
    batch = 8
    top, rest = halves_np(
        np.concatenate(list(shaped_taps(window_lags(), column_shapes, TAPS)), axis=1)
    )
    groups = batch // GROUP
    return pl.pallas_call(
        functools.partial(match_body, capacity),
        grid_spec=pltpu.PrefetchScalarGridSpec(
            num_scalar_prefetch=1,
            grid=(count // batch,),
            in_specs=[
                pl.BlockSpec((batch, rows, width), lambda i, r: (i, 0, 0)),
                pl.BlockSpec((groups,) + mix.shape[1:], lambda i, r: (i, 0, 0)),
                pl.BlockSpec(top.shape, lambda i, r: (0, 0)),
                pl.BlockSpec(rest.shape, lambda i, r: (0, 0)),
            ],
            out_specs=pl.BlockSpec((tiles * capacity, rows, width), lambda i, r: (0, 0, 0)),
            scratch_shapes=[pltpu.SMEM((tiles,), jnp.int32)],
        ),
        out_shape=jax.ShapeDtypeStruct((tiles * capacity, rows, width), F32),
        compiler_params=pltpu.CompilerParams(vmem_limit_bytes=50 * 2**20),
        name="match",
    )(routes, pieces, mix, top, rest)


def mix_table(coeffs, weights, rows):
    count, kinds_row, kinds = coeffs.shape
    lag = np.arange(rows)[None, :] - np.arange(rows)[:, None]
    bank = jnp.asarray(shaped_taps(lag, row_shapes, TAPS).astype(np.float32))
    weighted = coeffs * weights[:, None, None]
    each = jnp.einsum("mab,aqp->mqbp", weighted, bank, precision=highest)
    each = each.reshape(count // GROUP, GROUP, rows, kinds, 1, rows)
    same = np.eye(GROUP, dtype=bool)[None, :, None, None, :, None]
    return jnp.where(same, each, 0.0).reshape(
        count // GROUP, GROUP * rows, kinds * GROUP * rows
    )


def gather_body(spot_ref, landed_ref, out_ref):
    out_ref[...] = jnp.zeros_like(out_ref)

    @pl.loop(0, landed_ref.shape[0])
    def _(i):
        out_ref[spot_ref[i]] += landed_ref[i]


def scatter_add(landed, spots, blocks):
    slots, rows, width = landed.shape
    return pl.pallas_call(
        gather_body,
        grid_spec=pltpu.PrefetchScalarGridSpec(
            num_scalar_prefetch=1,
            grid=(1,),
            in_specs=[pl.BlockSpec(landed.shape, lambda i, r: (0, 0, 0))],
            out_specs=pl.BlockSpec((blocks, rows, width), lambda i, r: (0, 0, 0)),
        ),
        out_shape=jax.ShapeDtypeStruct((blocks, rows, width), F32),
        compiler_params=pltpu.CompilerParams(vmem_limit_bytes=50 * 2**20),
        name="scatter_add",
    )(spots, landed)


def detect_body(above_ref, here_ref, below_ref, top_ref, rest_ref, band_top_ref, band_rest_ref, out_ref):
    cells = jnp.concatenate([above_ref[...], here_ref[...], below_ref[...]], axis=0)
    rows, width = cells.shape
    top, rest = halves(windows_of(cells))
    swept = dot(top, top_ref[...]) + (dot(rest, top_ref[...]) + dot(top, rest_ref[...]))
    sheet = jnp.concatenate(
        [swept[j * rows : (j + 1) * rows] for j in range(width // LANES)], axis=1
    )
    s_top, s_rest = halves(sheet)
    b_top, b_rest = band_top_ref[...], band_rest_ref[...]
    out_ref[...] = dot(b_top, s_top) + (dot(b_rest, s_top) + dot(b_top, s_rest))


def detect(above, here, below):
    rows = here.shape[0]
    top, rest = halves_np(detect_taps(window_lags(), REACH))
    lag = np.arange(rows + 2 * RIM)[None, :] - RIM - np.arange(rows)[:, None]
    band_top, band_rest = halves_np(detect_taps(lag, REACH))
    return pl.pallas_call(
        detect_body,
        out_shape=jax.ShapeDtypeStruct(here.shape, F32),
        compiler_params=pltpu.CompilerParams(vmem_limit_bytes=50 * 2**20),
        name="detect",
    )(above, here, below, top, rest, band_top, band_rest)


def shards(pieces, coeffs, weights, routes, offsets):
    tiles, quarters = lax.axis_size("tile"), lax.axis_size("vis")
    me_tile, me_vis = lax.axis_index("tile"), lax.axis_index("vis")
    count, rows, width = pieces.shape
    capacity = max(2, 2 * count // tiles)
    blocks = SR // rows
    target = routes[:, 0]
    facts = jnp.stack([target.astype(F32), offsets.astype(F32), weights])
    known = lax.all_gather(facts, ("tile", "vis"))
    sent = match(pieces, mix_table(coeffs, weights, rows), target, tiles, capacity)
    sent = sent.reshape(tiles, capacity, rows, width)
    landed = lax.all_to_all(sent, "tile", split_axis=0, concat_axis=0, tiled=True)
    landed = landed.reshape(tiles * capacity, rows, width)
    mine = known[:, 0] == me_tile.astype(F32)
    grid_of = jnp.arange(blocks).astype(F32)
    near_vis = lax.dynamic_slice_in_dim(
        known.reshape(tiles, quarters, 3, count), me_vis, 1, 1
    )[:, 0]
    hit = near_vis[:, 0] == me_tile.astype(F32)
    earlier = np.arange(count)[None, :] < np.arange(count)[:, None]
    rank = jnp.sum(jnp.where(earlier[None] & hit[:, None, :], 1, 0), axis=2)
    slot_hit = hit[:, None, :] & (rank[:, None, :] == jnp.arange(capacity)[None, :, None])
    spots = jnp.sum(jnp.where(slot_hit, near_vis[:, None, 1], 0.0), axis=2)
    spots = spots.astype(jnp.int32).reshape(-1)
    own_blocks = blocks // quarters
    own_grid = (me_vis * own_blocks + jnp.arange(own_blocks)).astype(F32)
    on_block = mine[None] & (known[:, 1][None] == own_grid[:, None, None])
    masses = jnp.sum(jnp.where(on_block, known[:, 2][None], 0.0), axis=(1, 2))
    inverse = jnp.where(masses > 0.0, 1.0 / jnp.where(masses > 0.0, masses, 1.0), 0.0)
    numerator = scatter_add(landed, spots, blocks)
    summed = lax.psum_scatter(numerator, "vis", scatter_dimension=0, tiled=True)
    coadd = jnp.where(
        (masses > 0.0)[:, None, None], summed * inverse[:, None, None], 0.0
    ).reshape(own_blocks * rows, width)
    total = tiles * quarters
    both = ("tile", "vis")
    above = lax.ppermute(coadd[-RIM:], both, [(i, i + 1) for i in range(total - 1)])
    below = lax.ppermute(coadd[:RIM], both, [(i + 1, i) for i in range(total - 1)])
    return coadd, detect(above, coadd, below)


def solution(mesh):
    placed = (
        P(("tile", "vis"), None, None),
        P(("tile", "vis"), None, None),
        P(("tile", "vis")),
        P(("tile", "vis"), None),
        P(("tile", "vis")),
    )
    return jax.shard_map(
        shards,
        mesh=mesh,
        in_specs=placed,
        out_specs=(P(("tile", "vis"), None), P(("tile", "vis"), None)),
        check_vma=False,
    )
```

```python
import functools

import jax
import jax.numpy as jnp
import ml_dtypes
import numpy as np
from jax import lax
from jax.experimental import pallas as pl
from jax.experimental.pallas import tpu as pltpu
from jax.sharding import PartitionSpec as P

SR = 1024
TAPS = 10
REACH = 15
LANES = 128
SIDE = 64
RIM = 16
GROUP = 4
CHUNK = 256

row_shapes = ((1.0, 0), (1.0, 1), (2.0, 0), (2.0, 2), (3.5, 0))
column_shapes = ((1.0, 0), (2.0, 0), (2.0, 1), (3.5, 0))
highest = lax.Precision.HIGHEST
F32 = jnp.float32
BF16 = jnp.bfloat16


def shaped_taps(lags, shapes, reach):
    spots = np.arange(-reach, reach + 1).astype(np.float64)
    lags = lags.astype(np.float64)
    stacked = []
    for spread, degree in shapes:
        full = np.exp(-spots * spots / (2.0 * spread * spread)) * (spots / spread) ** degree
        values = np.exp(-lags * lags / (2.0 * spread * spread)) * (lags / spread) ** degree
        values = values / np.sqrt(np.sum(full * full))
        stacked.append(np.where(np.abs(lags) <= reach, values, 0.0))
    return np.stack(stacked)


def detect_taps(lags, reach):
    spots = np.arange(-reach, reach + 1).astype(np.float64)
    total = np.sum(np.exp(-spots * spots / 18.0))
    lags = lags.astype(np.float64)
    values = np.exp(-lags * lags / 18.0) / total - 1.0 / (2 * reach + 1)
    return np.where(np.abs(lags) <= reach, values, 0.0)


def halves_np(table):
    table = table.astype(np.float32)
    top = table.astype(ml_dtypes.bfloat16)
    rest = (table - top.astype(np.float32)).astype(ml_dtypes.bfloat16)
    return jnp.asarray(top), jnp.asarray(rest)


def halves(x):
    top = x.astype(BF16)
    return top, (x - top.astype(F32)).astype(BF16)


def dot(a, b):
    return jnp.dot(a, b, preferred_element_type=F32)


def window_lags():
    return np.arange(2 * SIDE + LANES)[:, None] - SIDE - np.arange(LANES)[None, :]


def windows_of(x):
    rows, width = x.shape
    rim = jnp.zeros((rows, SIDE), x.dtype)
    padded = jnp.concatenate([rim, x, rim], axis=1)
    blocks = width // LANES
    return jnp.concatenate(
        [padded[:, LANES * j : LANES * (j + 2)] for j in range(blocks)], axis=0
    )


def match_body(capacity, routes_ref, pieces_ref, mix_ref, top_ref, rest_ref, out_ref, count_ref):
    step = pl.program_id(0)
    pieces, rows, width = pieces_ref.shape
    kinds = top_ref.shape[1] // LANES
    blocks = width // LANES

    @pl.when(step == 0)
    def _():
        out_ref[...] = jnp.zeros_like(out_ref)

        @pl.loop(0, count_ref.shape[0])
        def _(i):
            count_ref[i] = 0

    flat = pieces_ref[...].reshape(pieces * rows, width)
    wide = windows_of(flat)
    top, rest = halves(wide)
    swept = dot(top, top_ref[...]) + (dot(rest, top_ref[...]) + dot(top, rest_ref[...]))
    span = GROUP * rows
    for q in range(pieces // GROUP):
        parts = []
        for j in range(blocks):
            at = j * pieces * rows + q * span
            parts.append(
                jnp.concatenate(
                    [swept[at : at + span, LANES * b : LANES * (b + 1)] for b in range(kinds)],
                    axis=0,
                )
            )
        banked = jnp.concatenate(parts, axis=1)
        y_top, y_rest = halves(banked)
        m_top, m_rest = halves(mix_ref[q])
        result = dot(m_top, y_top) + (dot(m_rest, y_top) + dot(m_top, y_rest))
        for i in range(GROUP):
            strip = routes_ref[step * pieces + q * GROUP + i]
            rank = count_ref[strip]
            count_ref[strip] = rank + 1
            for c in range(out_ref.shape[0]):
                out_ref[c, strip * capacity + rank] = result[
                    i * rows : (i + 1) * rows, c * CHUNK : (c + 1) * CHUNK
                ]


def match(pieces, mix, routes, tiles, capacity):
    count, rows, width = pieces.shape
    batch = 8
    top, rest = halves_np(
        np.concatenate(list(shaped_taps(window_lags(), column_shapes, TAPS)), axis=1)
    )
    groups = batch // GROUP
    shape = (width // CHUNK, tiles * capacity, rows, CHUNK)
    return pl.pallas_call(
        functools.partial(match_body, capacity),
        grid_spec=pltpu.PrefetchScalarGridSpec(
            num_scalar_prefetch=1,
            grid=(count // batch,),
            in_specs=[
                pl.BlockSpec((batch, rows, width), lambda i, r: (i, 0, 0)),
                pl.BlockSpec((groups,) + mix.shape[1:], lambda i, r: (i, 0, 0)),
                pl.BlockSpec(top.shape, lambda i, r: (0, 0)),
                pl.BlockSpec(rest.shape, lambda i, r: (0, 0)),
            ],
            out_specs=pl.BlockSpec(shape, lambda i, r: (0, 0, 0, 0)),
            scratch_shapes=[pltpu.SMEM((tiles,), jnp.int32)],
        ),
        out_shape=jax.ShapeDtypeStruct(shape, F32),
        compiler_params=pltpu.CompilerParams(vmem_limit_bytes=50 * 2**20),
        name="match",
    )(routes, pieces, mix, top, rest)


def mix_table(coeffs, weights, rows):
    count, kinds_row, kinds = coeffs.shape
    lag = np.arange(rows)[None, :] - np.arange(rows)[:, None]
    bank = jnp.asarray(shaped_taps(lag, row_shapes, TAPS).astype(np.float32))
    weighted = coeffs * weights[:, None, None]
    each = jnp.einsum("mab,aqp->mqbp", weighted, bank, precision=highest)
    each = each.reshape(count // GROUP, GROUP, rows, kinds, 1, rows)
    same = np.eye(GROUP, dtype=bool)[None, :, None, None, :, None]
    return jnp.where(same, each, 0.0).reshape(
        count // GROUP, GROUP * rows, kinds * GROUP * rows
    )


def combine_body(
    tiles, quarters, spot_ref, inverse_ref, sent_ref, top_ref, rest_ref, band_top_ref, band_rest_ref,
    coadd_ref, out_ref,
    landed, select, part, right, left, sheet,
    ring_send, ring_recv, right_send, right_recv, left_send, left_recv, rim_send, rim_recv,
):
    tile, vis = lax.axis_index("tile"), lax.axis_index("vis")
    chunks, _, span, chunk = landed.shape
    slots = tiles * span
    strip = select.shape[0]
    own = strip // quarters
    first, last = vis == 0, vis == quarters - 1
    down = (
        lax.select(first, tile - 1, tile),
        lax.select(first, quarters - 1, vis - 1),
    )
    up = (lax.select(last, tile + 1, tile), lax.select(last, 0, vis + 1))
    has_down = jnp.logical_or(tile > 0, vis > 0)
    has_up = jnp.logical_or(tile < tiles - 1, vis < quarters - 1)

    barrier = pltpu.get_barrier_semaphore()

    def greet(device):
        pl.semaphore_signal(barrier, inc=1, device_id=device, device_id_type=pl.DeviceIdType.MESH)

    @pl.loop(1, tiles)
    def _(k):
        greet((lax.rem(tile + k, tiles), vis))

    @pl.when(has_down)
    def _():
        greet(down)

    @pl.when(has_up)
    def _():
        greet(up)

    pl.semaphore_wait(
        barrier, tiles - 1 + has_down.astype(jnp.int32) + has_up.astype(jnp.int32)
    )

    def ring(c, k):
        peer = lax.rem(tile + k, tiles)
        return pltpu.make_async_remote_copy(
            src_ref=sent_ref.at[c, peer],
            dst_ref=landed.at[c, tile],
            send_sem=ring_send.at[c, k],
            recv_sem=ring_recv.at[c, k],
            device_id=(peer, vis),
            device_id_type=pl.DeviceIdType.MESH,
        )

    def ring_arrival(c, k):
        peer = lax.rem(tile + tiles - k, tiles)
        return pltpu.make_async_remote_copy(
            src_ref=sent_ref.at[c, peer],
            dst_ref=landed.at[c, peer],
            send_sem=ring_send.at[c, k],
            recv_sem=ring_recv.at[c, k],
            device_id=(peer, vis),
            device_id_type=pl.DeviceIdType.MESH,
        )

    @pl.loop(0, chunks)
    def _(c):
        @pl.loop(1, tiles)
        def _(k):
            ring(c, k).start()

    spots = lax.broadcasted_iota(jnp.int32, (own, slots), 0)
    for q in range(quarters):
        select[q * own : (q + 1) * own] = jnp.where(
            spots + q * own == spot_ref[...], 1.0, 0.0
        ).astype(BF16)
    edge = jnp.zeros((chunks, RIM, chunk), F32)

    @pl.when(jnp.logical_not(has_down))
    def _():
        sheet[:, 0:RIM] = edge

    @pl.when(jnp.logical_not(has_up))
    def _():
        sheet[:, RIM + own : 2 * RIM + own] = edge

    def hop(held, c, q, sends, recvs, step, source):
        return pltpu.make_async_remote_copy(
            src_ref=source.at[c, q],
            dst_ref=held.at[c, q],
            send_sem=sends.at[c, q],
            recv_sem=recvs.at[c, q],
            device_id=(tile, vis + step),
            device_id_type=pl.DeviceIdType.MESH,
        )

    def forward(c, rightward):
        held, sends, recvs, step = (
            (right, right_send, right_recv, 1) if rightward else (left, left_send, left_recv, -1)
        )
        opens = first if rightward else last
        order = reversed(range(quarters)) if rightward else range(quarters)
        for q in order:
            beyond = vis < q if rightward else vis > q

            @pl.when(jnp.logical_and(beyond, opens))
            def _():
                hop(held, c, q, sends, recvs, step, part).start()

            @pl.when(jnp.logical_and(beyond, jnp.logical_not(opens)))
            def _():
                hop(held, c, q, sends, recvs, step, held).wait_recv()
                held[c, q] += part[c, q]
                hop(held, c, q, sends, recvs, step, held).start()

    def rim(c, upward):
        src = sheet.at[c, pl.ds(own, RIM)] if upward else sheet.at[c, pl.ds(RIM, RIM)]
        dst = sheet.at[c, pl.ds(0, RIM)] if upward else sheet.at[c, pl.ds(RIM + own, RIM)]
        way = 0 if upward else 1
        return pltpu.make_async_remote_copy(
            src_ref=src,
            dst_ref=dst,
            send_sem=rim_send.at[c, way],
            recv_sem=rim_recv.at[c, way],
            device_id=up if upward else down,
            device_id_type=pl.DeviceIdType.MESH,
        )

    @pl.loop(0, chunks + quarters - 1)
    def _(turn):
        @pl.when(turn < chunks)
        def _():
            c = turn

            @pl.loop(1, tiles)
            def _(k):
                ring_arrival(c, k).wait_recv()

            landed[c, tile] = sent_ref[c, tile]
            top, rest = halves(landed[c].reshape(slots, chunk))

            @pl.loop(0, quarters)
            def _(q):
                rows = select[pl.ds(pl.multiple_of(q * own, own), own), :]
                part[c, q] = dot(rows, top) + dot(rows, rest)

        for stage in range(quarters - 1):
            c = turn - stage

            @pl.when(jnp.logical_and(c >= 0, c < chunks))
            def _():
                @pl.when(vis == stage)
                def _():
                    forward(c, True)

                @pl.when(vis == quarters - 1 - stage)
                def _():
                    forward(c, False)

        c = turn - (quarters - 1)

        @pl.when(c >= 0)
        def _():
            total = part[c, vis]
            sheet[c, RIM : RIM + own] = total

            @pl.when(vis > 0)
            def _():
                hop(right, c, vis, right_send, right_recv, 0, part).wait_recv()
                sheet[c, RIM : RIM + own] += right[c, vis]

            @pl.when(vis < quarters - 1)
            def _():
                hop(left, c, vis, left_send, left_recv, 0, part).wait_recv()
                sheet[c, RIM : RIM + own] += left[c, vis]

            sheet[c, RIM : RIM + own] *= inverse_ref[...]

            @pl.when(has_up)
            def _():
                rim(c, True).start()

            @pl.when(has_down)
            def _():
                rim(c, False).start()

    for c in range(chunks):
        coadd_ref[:, c * chunk : (c + 1) * chunk] = sheet[c, RIM : RIM + own]

        @pl.when(has_down)
        def _():
            rim(c, True).wait_recv()

        @pl.when(has_up)
        def _():
            rim(c, False).wait_recv()

    b_top, b_rest = band_top_ref[...], band_rest_ref[...]
    columns = []
    for c in range(chunks):
        s_top, s_rest = halves(sheet[c])
        columns.append(dot(b_top, s_top) + (dot(b_rest, s_top) + dot(b_top, s_rest)))
    top, rest = halves(windows_of(jnp.concatenate(columns, axis=1)))
    swept = dot(top, top_ref[...]) + (dot(rest, top_ref[...]) + dot(top, rest_ref[...]))
    for j in range(out_ref.shape[1] // LANES):
        out_ref[:, j * LANES : (j + 1) * LANES] = swept[j * own : (j + 1) * own]

    @pl.loop(0, chunks)
    def _(c):
        @pl.loop(1, tiles)
        def _(k):
            ring(c, k).wait_send()

        @pl.when(has_up)
        def _():
            rim(c, True).wait_send()

        @pl.when(has_down)
        def _():
            rim(c, False).wait_send()

        for q in range(quarters):

            @pl.when(vis < q)
            def _():
                hop(right, c, q, right_send, right_recv, 1, part).wait_send()

            @pl.when(vis > q)
            def _():
                hop(left, c, q, left_send, left_recv, -1, part).wait_send()


def combine(sent, spots, inverse, tiles, quarters):
    chunks, _, span, chunk = sent.shape
    width = chunks * chunk
    own = SR // quarters
    top, rest = halves_np(detect_taps(window_lags(), REACH))
    lag = np.arange(own + 2 * RIM)[None, :] - RIM - np.arange(own)[:, None]
    band_top, band_rest = halves_np(detect_taps(lag, REACH))
    result = jax.ShapeDtypeStruct((own, width), F32)
    held = pltpu.VMEM((chunks, quarters, own, chunk), F32)
    pair = pltpu.SemaphoreType.DMA((chunks, tiles))
    step = pltpu.SemaphoreType.DMA((chunks, quarters))
    side = pltpu.SemaphoreType.DMA((chunks, 2))
    return pl.pallas_call(
        functools.partial(combine_body, tiles, quarters),
        out_shape=(result, result),
        in_specs=[pl.BlockSpec(memory_space=pltpu.VMEM)] * 7,
        out_specs=[pl.BlockSpec(memory_space=pltpu.VMEM)] * 2,
        scratch_shapes=[
            pltpu.VMEM(sent.shape, F32),
            pltpu.VMEM((SR, tiles * span), BF16),
            held,
            held,
            held,
            pltpu.VMEM((chunks, own + 2 * RIM, chunk), F32),
            pair, pair, step, step, step, step, side, side,
        ],
        compiler_params=pltpu.CompilerParams(
            vmem_limit_bytes=52 * 2**20, collective_id=0, has_side_effects=True
        ),
        name="combine",
    )(spots, inverse, sent, top, rest, band_top, band_rest)


def shards(pieces, coeffs, weights, routes, offsets):
    tiles, quarters = lax.axis_size("tile"), lax.axis_size("vis")
    me_tile, me_vis = lax.axis_index("tile"), lax.axis_index("vis")
    count, rows, width = pieces.shape
    capacity = max(2, 2 * count // tiles)
    blocks = SR // rows
    target = routes[:, 0]
    facts = jnp.stack([target.astype(F32), offsets.astype(F32), weights])
    known = lax.all_gather(facts, ("tile", "vis"))
    sent = match(pieces, mix_table(coeffs, weights, rows), target, tiles, capacity)
    sent = sent.reshape(width // CHUNK, tiles, capacity * rows, CHUNK)
    mine = known[:, 0] == me_tile.astype(F32)
    grid_of = jnp.arange(blocks).astype(F32)
    near_vis = lax.dynamic_slice_in_dim(
        known.reshape(tiles, quarters, 3, count), me_vis, 1, 1
    )[:, 0]
    hit = near_vis[:, 0] == me_tile.astype(F32)
    earlier = np.arange(count)[None, :] < np.arange(count)[:, None]
    rank = jnp.sum(jnp.where(earlier[None] & hit[:, None, :], 1, 0), axis=2)
    slot_hit = hit[:, None, :] & (rank[:, None, :] == jnp.arange(capacity)[None, :, None])
    spots = jnp.sum(jnp.where(slot_hit, near_vis[:, None, 1], 0.0), axis=2)
    spots = spots.astype(jnp.int32).reshape(-1, 1) * rows + jnp.arange(rows)
    own_blocks = blocks // quarters
    own_grid = (me_vis * own_blocks + jnp.arange(own_blocks)).astype(F32)
    on_block = mine[None] & (known[:, 1][None] == own_grid[:, None, None])
    masses = jnp.sum(jnp.where(on_block, known[:, 2][None], 0.0), axis=(1, 2))
    inverse = jnp.where(masses > 0.0, 1.0 / jnp.where(masses > 0.0, masses, 1.0), 0.0)
    inverse = jnp.broadcast_to(inverse[:, None, None], (own_blocks, rows, CHUNK))
    return combine(sent, spots.reshape(1, -1), inverse.reshape(-1, CHUNK), tiles, quarters)


def solution(mesh):
    placed = (
        P(("tile", "vis"), None, None),
        P(("tile", "vis"), None, None),
        P(("tile", "vis")),
        P(("tile", "vis"), None),
        P(("tile", "vis")),
    )
    return jax.shard_map(
        shards,
        mesh=mesh,
        in_specs=placed,
        out_specs=(P(("tile", "vis"), None), P(("tile", "vis"), None)),
        check_vma=False,
    )
```

```python
import functools

import jax
import jax.numpy as jnp
import ml_dtypes
import numpy as np
from jax import lax
from jax.experimental import pallas as pl
from jax.experimental.pallas import tpu as pltpu
from jax.sharding import PartitionSpec as P

SR = 1024
TAPS = 10
REACH = 15
LANES = 128
SIDE = 64
RIM = 16
GROUP = 4
CHUNK = 256

row_shapes = ((1.0, 0), (1.0, 1), (2.0, 0), (2.0, 2), (3.5, 0))
column_shapes = ((1.0, 0), (2.0, 0), (2.0, 1), (3.5, 0))
F32 = jnp.float32
BF16 = jnp.bfloat16


def shaped_taps(lags, shapes, reach):
    spots = np.arange(-reach, reach + 1).astype(np.float64)
    lags = lags.astype(np.float64)
    stacked = []
    for spread, degree in shapes:
        full = np.exp(-spots * spots / (2.0 * spread * spread)) * (spots / spread) ** degree
        values = np.exp(-lags * lags / (2.0 * spread * spread)) * (lags / spread) ** degree
        values = values / np.sqrt(np.sum(full * full))
        stacked.append(np.where(np.abs(lags) <= reach, values, 0.0))
    return np.stack(stacked)


def detect_taps(lags, reach):
    spots = np.arange(-reach, reach + 1).astype(np.float64)
    total = np.sum(np.exp(-spots * spots / 18.0))
    lags = lags.astype(np.float64)
    values = np.exp(-lags * lags / 18.0) / total - 1.0 / (2 * reach + 1)
    return np.where(np.abs(lags) <= reach, values, 0.0)


def halves_np(table):
    table = table.astype(np.float32)
    top = table.astype(ml_dtypes.bfloat16)
    rest = (table - top.astype(np.float32)).astype(ml_dtypes.bfloat16)
    return jnp.asarray(top), jnp.asarray(rest)


def halves(x):
    top = x.astype(BF16)
    return top, (x - top.astype(F32)).astype(BF16)


def dot(a, b):
    return jnp.dot(a, b, preferred_element_type=F32)


def window_lags():
    return np.arange(2 * SIDE + LANES)[:, None] - SIDE - np.arange(LANES)[None, :]


def windows_of(x):
    rows, width = x.shape
    rim = jnp.zeros((rows, SIDE), x.dtype)
    padded = jnp.concatenate([rim, x, rim], axis=1)
    blocks = width // LANES
    return jnp.concatenate(
        [padded[:, LANES * j : LANES * (j + 2)] for j in range(blocks)], axis=0
    )


def match_body(
    capacity, routes_ref, offsets_ref, weights_ref, coeffs_ref,
    pieces_ref, bank_ref, top_ref, rest_ref, out_ref, note_ref, count_ref,
):
    step = pl.program_id(0)
    pieces, rows, width = pieces_ref.shape
    kinds = top_ref.shape[1] // LANES
    blocks = width // LANES

    @pl.when(step == 0)
    def _():
        out_ref[...] = jnp.zeros_like(out_ref)
        note_ref[...] = jnp.full_like(note_ref, -1.0)

        @pl.loop(0, count_ref.shape[0])
        def _(i):
            count_ref[i] = 0

    flat = pieces_ref[...].reshape(pieces * rows, width)
    wide = windows_of(flat)
    top, rest = halves(wide)
    swept = dot(top, top_ref[...]) + (dot(rest, top_ref[...]) + dot(top, rest_ref[...]))
    span = GROUP * rows
    kinds_row, _, depth = bank_ref.shape
    lane = lax.broadcasted_iota(jnp.int32, (1, depth), 1)
    note_lane = lax.broadcasted_iota(jnp.int32, note_ref.shape[1:], 1)
    note_row = lax.broadcasted_iota(jnp.int32, note_ref.shape[1:], 0)

    def mix_of(piece, place):
        total = None
        for a in range(kinds_row):
            base = (piece * kinds_row + a) * kinds
            row = jnp.full((1, depth), coeffs_ref[base], F32)
            for b in range(1, kinds):
                row = jnp.where(lane >= b * span, coeffs_ref[base + b], row)
            term = row * bank_ref[a]
            total = term if total is None else total + term
        keep = jnp.logical_and(lane % span >= place * rows, lane % span < (place + 1) * rows)
        return jnp.where(keep, total * weights_ref[piece], 0.0)

    for q in range(pieces // GROUP):
        parts = []
        for j in range(blocks):
            at = j * pieces * rows + q * span
            parts.append(
                jnp.concatenate(
                    [swept[at : at + span, LANES * b : LANES * (b + 1)] for b in range(kinds)],
                    axis=0,
                )
            )
        banked = jnp.concatenate(parts, axis=1)
        y_top, y_rest = halves(banked)
        lead = step * pieces + q * GROUP
        m_top, m_rest = halves(
            jnp.concatenate([mix_of(lead + i, i) for i in range(GROUP)], axis=0)
        )
        result = dot(m_top, y_top) + (dot(m_rest, y_top) + dot(m_top, y_rest))
        for i in range(GROUP):
            piece = lead + i
            strip = routes_ref[piece]
            rank = count_ref[strip]
            count_ref[strip] = rank + 1
            fact = jnp.where(
                note_row == 0,
                (offsets_ref[piece] * rows + note_lane % rows).astype(F32),
                weights_ref[piece],
            )
            here = jnp.logical_and(note_lane >= rank * rows, note_lane < (rank + 1) * rows)
            note_ref[strip] = jnp.where(here, fact, note_ref[strip])
            for c in range(out_ref.shape[0]):
                out_ref[c, strip * capacity + rank] = result[
                    i * rows : (i + 1) * rows, c * CHUNK : (c + 1) * CHUNK
                ]


def match(pieces, coeffs, weights, routes, offsets, tiles, capacity):
    count, rows, width = pieces.shape
    batch = 8
    kinds = coeffs.shape[2]
    top, rest = halves_np(
        np.concatenate(list(shaped_taps(window_lags(), column_shapes, TAPS)), axis=1)
    )
    lag = np.arange(rows)[None, :] - np.arange(rows)[:, None]
    bank = np.tile(shaped_taps(lag, row_shapes, TAPS), (1, 1, kinds * GROUP)).astype(np.float32)
    shape = (width // CHUNK, tiles * capacity, rows, CHUNK)
    note = (tiles, 8, -(-capacity * rows // LANES) * LANES)
    return pl.pallas_call(
        functools.partial(match_body, capacity),
        grid_spec=pltpu.PrefetchScalarGridSpec(
            num_scalar_prefetch=4,
            grid=(count // batch,),
            in_specs=[
                pl.BlockSpec((batch, rows, width), lambda i, *r: (i, 0, 0)),
                pl.BlockSpec(bank.shape, lambda i, *r: (0, 0, 0)),
                pl.BlockSpec(top.shape, lambda i, *r: (0, 0)),
                pl.BlockSpec(rest.shape, lambda i, *r: (0, 0)),
            ],
            out_specs=[
                pl.BlockSpec(shape, lambda i, *r: (0, 0, 0, 0)),
                pl.BlockSpec(note, lambda i, *r: (0, 0, 0)),
            ],
            scratch_shapes=[pltpu.SMEM((tiles,), jnp.int32)],
        ),
        out_shape=(jax.ShapeDtypeStruct(shape, F32), jax.ShapeDtypeStruct(note, F32)),
        compiler_params=pltpu.CompilerParams(vmem_limit_bytes=50 * 2**20),
        name="match",
    )(routes, offsets, weights, coeffs.reshape(-1), pieces, jnp.asarray(bank), top, rest)


def combine_body(
    tiles, quarters, note_ref, sent_ref, top_ref, rest_ref, band_top_ref, band_rest_ref,
    coadd_ref, out_ref,
    landed, notes, select, part, right, left, sheet, inverse,
    note_send, note_recv, ring_send, ring_recv, right_send, right_recv, left_send, left_recv, rim_send, rim_recv,
):
    tile, vis = lax.axis_index("tile"), lax.axis_index("vis")
    chunks, _, span, chunk = landed.shape
    slots = tiles * span
    strip = select.shape[0]
    own = strip // quarters
    first, last = vis == 0, vis == quarters - 1
    down = (
        lax.select(first, tile - 1, tile),
        lax.select(first, quarters - 1, vis - 1),
    )
    up = (lax.select(last, tile + 1, tile), lax.select(last, 0, vis + 1))
    has_down = jnp.logical_or(tile > 0, vis > 0)
    has_up = jnp.logical_or(tile < tiles - 1, vis < quarters - 1)

    barrier = pltpu.get_barrier_semaphore()

    def greet(device):
        pl.semaphore_signal(barrier, inc=1, device_id=device, device_id_type=pl.DeviceIdType.MESH)

    everyone = tiles * quarters
    me = tile * quarters + vis

    @pl.loop(1, everyone)
    def _(k):
        peer = lax.rem(me + k, everyone)
        greet((lax.div(peer, quarters), lax.rem(peer, quarters)))

    pl.semaphore_wait(barrier, everyone - 1)

    def tell(k):
        peer = lax.rem(me + k, everyone)
        return pltpu.make_async_remote_copy(
            src_ref=note_ref.at[lax.div(peer, quarters)],
            dst_ref=notes.at[vis, tile],
            send_sem=note_send.at[k],
            recv_sem=note_recv.at[k],
            device_id=(lax.div(peer, quarters), lax.rem(peer, quarters)),
            device_id_type=pl.DeviceIdType.MESH,
        )

    def told(k):
        peer = lax.rem(me + everyone - k, everyone)
        return pltpu.make_async_remote_copy(
            src_ref=note_ref.at[lax.div(peer, quarters)],
            dst_ref=notes.at[lax.rem(peer, quarters), lax.div(peer, quarters)],
            send_sem=note_send.at[k],
            recv_sem=note_recv.at[k],
            device_id=(lax.div(peer, quarters), lax.rem(peer, quarters)),
            device_id_type=pl.DeviceIdType.MESH,
        )

    @pl.loop(1, everyone)
    def _(k):
        tell(k).start()

    def ring(c, k):
        peer = lax.rem(tile + k, tiles)
        return pltpu.make_async_remote_copy(
            src_ref=sent_ref.at[c, peer],
            dst_ref=landed.at[c, tile],
            send_sem=ring_send.at[c, k],
            recv_sem=ring_recv.at[c, k],
            device_id=(peer, vis),
            device_id_type=pl.DeviceIdType.MESH,
        )

    def ring_arrival(c, k):
        peer = lax.rem(tile + tiles - k, tiles)
        return pltpu.make_async_remote_copy(
            src_ref=sent_ref.at[c, peer],
            dst_ref=landed.at[c, peer],
            send_sem=ring_send.at[c, k],
            recv_sem=ring_recv.at[c, k],
            device_id=(peer, vis),
            device_id_type=pl.DeviceIdType.MESH,
        )

    @pl.loop(0, chunks)
    def _(c):
        @pl.loop(1, tiles)
        def _(k):
            ring(c, k).start()

    notes[vis, tile] = note_ref[tile]

    @pl.loop(1, everyone)
    def _(k):
        told(k).wait_recv()

    grid_rows = lax.broadcasted_iota(jnp.int32, (own, slots), 0).astype(F32)
    spots = jnp.concatenate([notes[vis, t, 0:1, 0:span] for t in range(tiles)], axis=1)
    for q in range(quarters):
        select[q * own : (q + 1) * own] = jnp.where(grid_rows + q * own == spots, 1.0, 0.0).astype(BF16)
    own_rows = lax.broadcasted_iota(jnp.int32, (own, span), 0) + vis * own
    own_rows = own_rows.astype(F32)

    def weigh(i, total):
        v, t = lax.rem(i, quarters), lax.div(i, quarters)
        hit = own_rows == notes[v, t, 0:1, 0:span]
        return total + jnp.where(hit, notes[v, t, 1:2, 0:span], 0.0)

    masses = lax.fori_loop(0, everyone, weigh, jnp.zeros((own, span), F32))
    mass = jnp.sum(masses, axis=1, keepdims=True)
    scale = jnp.where(mass > 0.0, 1.0 / jnp.where(mass > 0.0, mass, 1.0), 0.0)
    inverse[...] = jnp.broadcast_to(scale, (own, LANES))
    edge = jnp.zeros((chunks, RIM, chunk), F32)

    @pl.when(jnp.logical_not(has_down))
    def _():
        sheet[:, 0:RIM] = edge

    @pl.when(jnp.logical_not(has_up))
    def _():
        sheet[:, RIM + own : 2 * RIM + own] = edge

    def hop(held, c, q, sends, recvs, step, source):
        return pltpu.make_async_remote_copy(
            src_ref=source.at[c, q],
            dst_ref=held.at[c, q],
            send_sem=sends.at[c, q],
            recv_sem=recvs.at[c, q],
            device_id=(tile, vis + step),
            device_id_type=pl.DeviceIdType.MESH,
        )

    def forward(c, rightward):
        held, sends, recvs, step = (
            (right, right_send, right_recv, 1) if rightward else (left, left_send, left_recv, -1)
        )
        opens = first if rightward else last
        order = reversed(range(quarters)) if rightward else range(quarters)
        for q in order:
            beyond = vis < q if rightward else vis > q

            @pl.when(jnp.logical_and(beyond, opens))
            def _():
                hop(held, c, q, sends, recvs, step, part).start()

            @pl.when(jnp.logical_and(beyond, jnp.logical_not(opens)))
            def _():
                hop(held, c, q, sends, recvs, step, held).wait_recv()
                held[c, q] += part[c, q]
                hop(held, c, q, sends, recvs, step, held).start()

    def rim(c, upward):
        src = sheet.at[c, pl.ds(own, RIM)] if upward else sheet.at[c, pl.ds(RIM, RIM)]
        dst = sheet.at[c, pl.ds(0, RIM)] if upward else sheet.at[c, pl.ds(RIM + own, RIM)]
        way = 0 if upward else 1
        return pltpu.make_async_remote_copy(
            src_ref=src,
            dst_ref=dst,
            send_sem=rim_send.at[c, way],
            recv_sem=rim_recv.at[c, way],
            device_id=up if upward else down,
            device_id_type=pl.DeviceIdType.MESH,
        )

    @pl.loop(0, chunks + quarters - 1)
    def _(turn):
        @pl.when(turn < chunks)
        def _():
            c = turn

            @pl.loop(1, tiles)
            def _(k):
                ring_arrival(c, k).wait_recv()

            landed[c, tile] = sent_ref[c, tile]
            top, rest = halves(landed[c].reshape(slots, chunk))

            @pl.loop(0, quarters)
            def _(q):
                rows = select[pl.ds(pl.multiple_of(q * own, own), own), :]
                part[c, q] = dot(rows, top) + dot(rows, rest)

        for stage in range(quarters - 1):
            c = turn - stage

            @pl.when(jnp.logical_and(c >= 0, c < chunks))
            def _():
                @pl.when(vis == stage)
                def _():
                    forward(c, True)

                @pl.when(vis == quarters - 1 - stage)
                def _():
                    forward(c, False)

        c = turn - (quarters - 1)

        @pl.when(c >= 0)
        def _():
            total = part[c, vis]
            sheet[c, RIM : RIM + own] = total

            @pl.when(vis > 0)
            def _():
                hop(right, c, vis, right_send, right_recv, 0, part).wait_recv()
                sheet[c, RIM : RIM + own] += right[c, vis]

            @pl.when(vis < quarters - 1)
            def _():
                hop(left, c, vis, left_send, left_recv, 0, part).wait_recv()
                sheet[c, RIM : RIM + own] += left[c, vis]

            for j in range(chunk // LANES):
                sheet[c, RIM : RIM + own, j * LANES : (j + 1) * LANES] *= inverse[...]

            @pl.when(has_up)
            def _():
                rim(c, True).start()

            @pl.when(has_down)
            def _():
                rim(c, False).start()

    for c in range(chunks):
        coadd_ref[:, c * chunk : (c + 1) * chunk] = sheet[c, RIM : RIM + own]

        @pl.when(has_down)
        def _():
            rim(c, True).wait_recv()

        @pl.when(has_up)
        def _():
            rim(c, False).wait_recv()

    b_top, b_rest = band_top_ref[...], band_rest_ref[...]
    columns = []
    for c in range(chunks):
        s_top, s_rest = halves(sheet[c])
        columns.append(dot(b_top, s_top) + (dot(b_rest, s_top) + dot(b_top, s_rest)))
    top, rest = halves(windows_of(jnp.concatenate(columns, axis=1)))
    swept = dot(top, top_ref[...]) + (dot(rest, top_ref[...]) + dot(top, rest_ref[...]))
    for j in range(out_ref.shape[1] // LANES):
        out_ref[:, j * LANES : (j + 1) * LANES] = swept[j * own : (j + 1) * own]

    @pl.loop(1, everyone)
    def _(k):
        tell(k).wait_send()

    @pl.loop(0, chunks)
    def _(c):
        @pl.loop(1, tiles)
        def _(k):
            ring(c, k).wait_send()

        @pl.when(has_up)
        def _():
            rim(c, True).wait_send()

        @pl.when(has_down)
        def _():
            rim(c, False).wait_send()

        for q in range(quarters):

            @pl.when(vis < q)
            def _():
                hop(right, c, q, right_send, right_recv, 1, part).wait_send()

            @pl.when(vis > q)
            def _():
                hop(left, c, q, left_send, left_recv, -1, part).wait_send()


def combine(sent, note, tiles, quarters):
    chunks, _, span, chunk = sent.shape
    width = chunks * chunk
    own = SR // quarters
    top, rest = halves_np(detect_taps(window_lags(), REACH))
    lag = np.arange(own + 2 * RIM)[None, :] - RIM - np.arange(own)[:, None]
    band_top, band_rest = halves_np(detect_taps(lag, REACH))
    result = jax.ShapeDtypeStruct((own, width), F32)
    held = pltpu.VMEM((chunks, quarters, own, chunk), F32)
    every = pltpu.SemaphoreType.DMA((tiles * quarters,))
    pair = pltpu.SemaphoreType.DMA((chunks, tiles))
    step = pltpu.SemaphoreType.DMA((chunks, quarters))
    side = pltpu.SemaphoreType.DMA((chunks, 2))
    return pl.pallas_call(
        functools.partial(combine_body, tiles, quarters),
        out_shape=(result, result),
        in_specs=[pl.BlockSpec(memory_space=pltpu.VMEM)] * 6,
        out_specs=[pl.BlockSpec(memory_space=pltpu.VMEM)] * 2,
        scratch_shapes=[
            pltpu.VMEM(sent.shape, F32),
            pltpu.VMEM((quarters,) + note.shape, F32),
            pltpu.VMEM((SR, tiles * span), BF16),
            held,
            held,
            held,
            pltpu.VMEM((chunks, own + 2 * RIM, chunk), F32),
            pltpu.VMEM((own, LANES), F32),
            every, every, pair, pair, step, step, step, step, side, side,
        ],
        compiler_params=pltpu.CompilerParams(
            vmem_limit_bytes=52 * 2**20, collective_id=0, has_side_effects=True
        ),
        name="combine",
    )(note, sent, top, rest, band_top, band_rest)


def shards(pieces, coeffs, weights, routes, offsets):
    tiles, quarters = lax.axis_size("tile"), lax.axis_size("vis")
    count, rows, width = pieces.shape
    capacity = max(2, 2 * count // tiles)
    sent, note = match(pieces, coeffs, weights, routes[:, 0], offsets, tiles, capacity)
    sent = sent.reshape(width // CHUNK, tiles, capacity * rows, CHUNK)
    return combine(sent, note, tiles, quarters)


def solution(mesh):
    placed = (
        P(("tile", "vis"), None, None),
        P(("tile", "vis"), None, None),
        P(("tile", "vis")),
        P(("tile", "vis"), None),
        P(("tile", "vis")),
    )
    return jax.shard_map(
        shards,
        mesh=mesh,
        in_specs=placed,
        out_specs=(P(("tile", "vis"), None), P(("tile", "vis"), None)),
        check_vma=False,
    )
```

```python
import functools

import jax
import jax.numpy as jnp
import ml_dtypes
import numpy as np
from jax import lax
from jax.experimental import pallas as pl
from jax.experimental.pallas import tpu as pltpu
from jax.sharding import PartitionSpec as P

SR = 1024
TAPS = 10
REACH = 15
LANES = 128
SIDE = 64
RIM = 16
GROUP = 4
CHUNK = 128

row_shapes = ((1.0, 0), (1.0, 1), (2.0, 0), (2.0, 2), (3.5, 0))
column_shapes = ((1.0, 0), (2.0, 0), (2.0, 1), (3.5, 0))
F32 = jnp.float32
BF16 = jnp.bfloat16


def shaped_taps(lags, shapes, reach):
    spots = np.arange(-reach, reach + 1).astype(np.float64)
    lags = lags.astype(np.float64)
    stacked = []
    for spread, degree in shapes:
        full = np.exp(-spots * spots / (2.0 * spread * spread)) * (spots / spread) ** degree
        values = np.exp(-lags * lags / (2.0 * spread * spread)) * (lags / spread) ** degree
        values = values / np.sqrt(np.sum(full * full))
        stacked.append(np.where(np.abs(lags) <= reach, values, 0.0))
    return np.stack(stacked)


def detect_taps(lags, reach):
    spots = np.arange(-reach, reach + 1).astype(np.float64)
    total = np.sum(np.exp(-spots * spots / 18.0))
    lags = lags.astype(np.float64)
    values = np.exp(-lags * lags / 18.0) / total - 1.0 / (2 * reach + 1)
    return np.where(np.abs(lags) <= reach, values, 0.0)


def halves_np(table):
    table = table.astype(np.float32)
    top = table.astype(ml_dtypes.bfloat16)
    rest = (table - top.astype(np.float32)).astype(ml_dtypes.bfloat16)
    return jnp.asarray(np.stack([top, rest]))


def halves(x):
    top = x.astype(BF16)
    return top, (x - top.astype(F32)).astype(BF16)


def dot(a, b):
    return jnp.dot(a, b, preferred_element_type=F32)


def window_lags():
    return np.arange(2 * SIDE + LANES)[:, None] - SIDE - np.arange(LANES)[None, :]


def windows_of(x):
    rows, width = x.shape
    rim = jnp.zeros((rows, SIDE), x.dtype)
    padded = jnp.concatenate([rim, x, rim], axis=1)
    blocks = width // LANES
    return jnp.concatenate(
        [padded[:, LANES * j : LANES * (j + 2)] for j in range(blocks)], axis=0
    )


def match_body(
    capacity, routes_ref, offsets_ref, weights_ref, coeffs_ref,
    pieces_ref, bank_ref, taps_ref, out_ref, note_ref, count_ref,
):
    step = pl.program_id(0)
    pieces, rows, width = pieces_ref.shape
    kinds = taps_ref.shape[2] // LANES
    blocks = width // LANES

    @pl.when(step == 0)
    def _():
        out_ref[...] = jnp.zeros_like(out_ref)
        note_ref[...] = jnp.full_like(note_ref, -1.0)

        @pl.loop(0, count_ref.shape[0])
        def _(i):
            count_ref[i] = 0

    flat = pieces_ref[...].reshape(pieces * rows, width)
    wide = windows_of(flat)
    top, rest = halves(wide)
    swept = dot(top, taps_ref[0]) + (dot(rest, taps_ref[0]) + dot(top, taps_ref[1]))
    span = GROUP * rows
    kinds_row, _, depth = bank_ref.shape
    lane = lax.broadcasted_iota(jnp.int32, (1, depth), 1)
    note_lane = lax.broadcasted_iota(jnp.int32, note_ref.shape[1:], 1)
    note_row = lax.broadcasted_iota(jnp.int32, note_ref.shape[1:], 0)

    def mix_of(piece, place):
        total = None
        for a in range(kinds_row):
            base = (piece * kinds_row + a) * kinds
            row = jnp.full((1, depth), coeffs_ref[base], F32)
            for b in range(1, kinds):
                row = jnp.where(lane >= b * span, coeffs_ref[base + b], row)
            term = row * bank_ref[a]
            total = term if total is None else total + term
        keep = jnp.logical_and(lane % span >= place * rows, lane % span < (place + 1) * rows)
        return jnp.where(keep, total * weights_ref[piece], 0.0)

    for q in range(pieces // GROUP):
        parts = []
        for j in range(blocks):
            at = j * pieces * rows + q * span
            parts.append(
                jnp.concatenate(
                    [swept[at : at + span, LANES * b : LANES * (b + 1)] for b in range(kinds)],
                    axis=0,
                )
            )
        banked = jnp.concatenate(parts, axis=1)
        y_top, y_rest = halves(banked)
        lead = step * pieces + q * GROUP
        m_top, m_rest = halves(
            jnp.concatenate([mix_of(lead + i, i) for i in range(GROUP)], axis=0)
        )
        result = dot(m_top, y_top) + (dot(m_rest, y_top) + dot(m_top, y_rest))
        for i in range(GROUP):
            piece = lead + i
            strip = routes_ref[piece]
            rank = count_ref[strip]
            count_ref[strip] = rank + 1
            fact = jnp.where(
                note_row == 0,
                (offsets_ref[piece] * rows + note_lane % rows).astype(F32),
                weights_ref[piece],
            )
            here = jnp.logical_and(note_lane >= rank * rows, note_lane < (rank + 1) * rows)
            note_ref[strip] = jnp.where(here, fact, note_ref[strip])
            for c in range(out_ref.shape[0]):
                out_ref[c, strip * capacity + rank] = result[
                    i * rows : (i + 1) * rows, c * CHUNK : (c + 1) * CHUNK
                ]


def match(pieces, coeffs, weights, routes, offsets, tiles, capacity):
    count, rows, width = pieces.shape
    batch = 8
    kinds = coeffs.shape[2]
    taps = halves_np(
        np.concatenate(list(shaped_taps(window_lags(), column_shapes, TAPS)), axis=1)
    )
    lag = np.arange(rows)[None, :] - np.arange(rows)[:, None]
    bank = np.tile(shaped_taps(lag, row_shapes, TAPS), (1, 1, kinds * GROUP)).astype(np.float32)
    shape = (width // CHUNK, tiles * capacity, rows, CHUNK)
    note = (tiles, 8, -(-capacity * rows // LANES) * LANES)
    return pl.pallas_call(
        functools.partial(match_body, capacity),
        grid_spec=pltpu.PrefetchScalarGridSpec(
            num_scalar_prefetch=4,
            grid=(count // batch,),
            in_specs=[
                pl.BlockSpec((batch, rows, width), lambda i, *r: (i, 0, 0)),
                pl.BlockSpec(bank.shape, lambda i, *r: (0, 0, 0)),
                pl.BlockSpec(taps.shape, lambda i, *r: (0, 0, 0)),
            ],
            out_specs=[
                pl.BlockSpec(shape, lambda i, *r: (0, 0, 0, 0)),
                pl.BlockSpec(note, lambda i, *r: (0, 0, 0)),
            ],
            scratch_shapes=[pltpu.SMEM((tiles,), jnp.int32)],
        ),
        out_shape=(jax.ShapeDtypeStruct(shape, F32), jax.ShapeDtypeStruct(note, F32)),
        compiler_params=pltpu.CompilerParams(vmem_limit_bytes=50 * 2**20),
        name="match",
    )(routes, offsets, weights, coeffs.reshape(-1), pieces, jnp.asarray(bank), taps)


def combine_body(
    tiles, quarters, note_ref, sent_ref, taps_ref, band_ref,
    coadd_ref, out_ref,
    landed, notes, select, part, right, left, sheet, inverse,
    note_send, note_recv, ring_send, ring_recv, right_send, right_recv, left_send, left_recv, rim_send, rim_recv,
):
    tile, vis = lax.axis_index("tile"), lax.axis_index("vis")
    chunks, _, span, chunk = landed.shape
    slots = tiles * span
    strip = select.shape[0]
    own = strip // quarters
    first, last = vis == 0, vis == quarters - 1
    down = (
        lax.select(first, tile - 1, tile),
        lax.select(first, quarters - 1, vis - 1),
    )
    up = (lax.select(last, tile + 1, tile), lax.select(last, 0, vis + 1))
    has_down = jnp.logical_or(tile > 0, vis > 0)
    has_up = jnp.logical_or(tile < tiles - 1, vis < quarters - 1)

    barrier = pltpu.get_barrier_semaphore()

    def greet(device):
        pl.semaphore_signal(barrier, inc=1, device_id=device, device_id_type=pl.DeviceIdType.MESH)

    everyone = tiles * quarters
    me = tile * quarters + vis

    @pl.loop(1, everyone)
    def _(k):
        peer = lax.rem(me + k, everyone)
        greet((lax.div(peer, quarters), lax.rem(peer, quarters)))

    pl.semaphore_wait(barrier, everyone - 1)

    def tell(k):
        peer = lax.rem(me + k, everyone)
        return pltpu.make_async_remote_copy(
            src_ref=note_ref.at[lax.div(peer, quarters)],
            dst_ref=notes.at[vis, tile],
            send_sem=note_send.at[k],
            recv_sem=note_recv.at[k],
            device_id=(lax.div(peer, quarters), lax.rem(peer, quarters)),
            device_id_type=pl.DeviceIdType.MESH,
        )

    def told(k):
        peer = lax.rem(me + everyone - k, everyone)
        return pltpu.make_async_remote_copy(
            src_ref=note_ref.at[lax.div(peer, quarters)],
            dst_ref=notes.at[lax.rem(peer, quarters), lax.div(peer, quarters)],
            send_sem=note_send.at[k],
            recv_sem=note_recv.at[k],
            device_id=(lax.div(peer, quarters), lax.rem(peer, quarters)),
            device_id_type=pl.DeviceIdType.MESH,
        )

    @pl.loop(1, everyone)
    def _(k):
        tell(k).start()

    def ring(c, k):
        peer = lax.rem(tile + k, tiles)
        return pltpu.make_async_remote_copy(
            src_ref=sent_ref.at[c, peer],
            dst_ref=landed.at[c, tile],
            send_sem=ring_send.at[c, k],
            recv_sem=ring_recv.at[c, k],
            device_id=(peer, vis),
            device_id_type=pl.DeviceIdType.MESH,
        )

    def ring_arrival(c, k):
        peer = lax.rem(tile + tiles - k, tiles)
        return pltpu.make_async_remote_copy(
            src_ref=sent_ref.at[c, peer],
            dst_ref=landed.at[c, peer],
            send_sem=ring_send.at[c, k],
            recv_sem=ring_recv.at[c, k],
            device_id=(peer, vis),
            device_id_type=pl.DeviceIdType.MESH,
        )

    @pl.loop(0, chunks)
    def _(c):
        @pl.loop(1, tiles)
        def _(k):
            ring(c, k).start()

    notes[vis, tile] = note_ref[tile]

    @pl.loop(1, everyone)
    def _(k):
        told(k).wait_recv()

    grid_rows = lax.broadcasted_iota(jnp.int32, (own, slots), 0).astype(F32)
    spots = jnp.concatenate([notes[vis, t, 0:1, 0:span] for t in range(tiles)], axis=1)
    for q in range(quarters):
        select[q * own : (q + 1) * own] = jnp.where(grid_rows + q * own == spots, 1.0, 0.0).astype(BF16)
    own_rows = lax.broadcasted_iota(jnp.int32, (own, span), 0) + vis * own
    own_rows = own_rows.astype(F32)

    def weigh(i, total):
        v, t = lax.rem(i, quarters), lax.div(i, quarters)
        hit = own_rows == notes[v, t, 0:1, 0:span]
        return total + jnp.where(hit, notes[v, t, 1:2, 0:span], 0.0)

    masses = lax.fori_loop(0, everyone, weigh, jnp.zeros((own, span), F32))
    mass = jnp.sum(masses, axis=1, keepdims=True)
    scale = jnp.where(mass > 0.0, 1.0 / jnp.where(mass > 0.0, mass, 1.0), 0.0)
    inverse[...] = jnp.broadcast_to(scale, (own, LANES))
    edge = jnp.zeros((chunks, RIM, chunk), F32)

    @pl.when(jnp.logical_not(has_down))
    def _():
        sheet[:, 0:RIM] = edge

    @pl.when(jnp.logical_not(has_up))
    def _():
        sheet[:, RIM + own : 2 * RIM + own] = edge

    def hop(held, c, q, sends, recvs, step, source):
        return pltpu.make_async_remote_copy(
            src_ref=source.at[c, q],
            dst_ref=held.at[c, q],
            send_sem=sends.at[c, q],
            recv_sem=recvs.at[c, q],
            device_id=(tile, vis + step),
            device_id_type=pl.DeviceIdType.MESH,
        )

    def forward(c, rightward):
        held, sends, recvs, step = (
            (right, right_send, right_recv, 1) if rightward else (left, left_send, left_recv, -1)
        )
        opens = first if rightward else last
        order = reversed(range(quarters)) if rightward else range(quarters)
        for q in order:
            beyond = vis < q if rightward else vis > q

            @pl.when(jnp.logical_and(beyond, opens))
            def _():
                hop(held, c, q, sends, recvs, step, part).start()

            @pl.when(jnp.logical_and(beyond, jnp.logical_not(opens)))
            def _():
                hop(held, c, q, sends, recvs, step, held).wait_recv()
                held[c, q] += part[c, q]
                hop(held, c, q, sends, recvs, step, held).start()

    def rim(c, upward):
        src = sheet.at[c, pl.ds(own, RIM)] if upward else sheet.at[c, pl.ds(RIM, RIM)]
        dst = sheet.at[c, pl.ds(0, RIM)] if upward else sheet.at[c, pl.ds(RIM + own, RIM)]
        way = 0 if upward else 1
        return pltpu.make_async_remote_copy(
            src_ref=src,
            dst_ref=dst,
            send_sem=rim_send.at[c, way],
            recv_sem=rim_recv.at[c, way],
            device_id=up if upward else down,
            device_id_type=pl.DeviceIdType.MESH,
        )

    @pl.loop(0, chunks + quarters - 1)
    def _(turn):
        @pl.when(turn < chunks)
        def _():
            c = turn

            @pl.loop(1, tiles)
            def _(k):
                ring_arrival(c, k).wait_recv()

            landed[c, tile] = sent_ref[c, tile]
            top, rest = halves(landed[c].reshape(slots, chunk))

            @pl.loop(0, quarters)
            def _(q):
                rows = select[pl.ds(pl.multiple_of(q * own, own), own), :]
                part[c, q] = dot(rows, top) + dot(rows, rest)

        for stage in range(quarters - 1):
            c = turn - stage

            @pl.when(jnp.logical_and(c >= 0, c < chunks))
            def _():
                @pl.when(vis == stage)
                def _():
                    forward(c, True)

                @pl.when(vis == quarters - 1 - stage)
                def _():
                    forward(c, False)

        c = turn - (quarters - 1)

        @pl.when(c >= 0)
        def _():
            total = part[c, vis]
            sheet[c, RIM : RIM + own] = total

            @pl.when(vis > 0)
            def _():
                hop(right, c, vis, right_send, right_recv, 0, part).wait_recv()
                sheet[c, RIM : RIM + own] += right[c, vis]

            @pl.when(vis < quarters - 1)
            def _():
                hop(left, c, vis, left_send, left_recv, 0, part).wait_recv()
                sheet[c, RIM : RIM + own] += left[c, vis]

            for j in range(chunk // LANES):
                sheet[c, RIM : RIM + own, j * LANES : (j + 1) * LANES] *= inverse[...]

            @pl.when(has_up)
            def _():
                rim(c, True).start()

            @pl.when(has_down)
            def _():
                rim(c, False).start()

    for c in range(chunks):
        coadd_ref[:, c * chunk : (c + 1) * chunk] = sheet[c, RIM : RIM + own]

        @pl.when(has_down)
        def _():
            rim(c, True).wait_recv()

        @pl.when(has_up)
        def _():
            rim(c, False).wait_recv()

    b_top, b_rest = band_ref[0], band_ref[1]
    columns = []
    for c in range(chunks):
        s_top, s_rest = halves(sheet[c])
        columns.append(dot(b_top, s_top) + (dot(b_rest, s_top) + dot(b_top, s_rest)))
    top, rest = halves(windows_of(jnp.concatenate(columns, axis=1)))
    swept = dot(top, taps_ref[0]) + (dot(rest, taps_ref[0]) + dot(top, taps_ref[1]))
    for j in range(out_ref.shape[1] // LANES):
        out_ref[:, j * LANES : (j + 1) * LANES] = swept[j * own : (j + 1) * own]

    @pl.loop(1, everyone)
    def _(k):
        tell(k).wait_send()

    @pl.loop(0, chunks)
    def _(c):
        @pl.loop(1, tiles)
        def _(k):
            ring(c, k).wait_send()

        @pl.when(has_up)
        def _():
            rim(c, True).wait_send()

        @pl.when(has_down)
        def _():
            rim(c, False).wait_send()

        for q in range(quarters):

            @pl.when(vis < q)
            def _():
                hop(right, c, q, right_send, right_recv, 1, part).wait_send()

            @pl.when(vis > q)
            def _():
                hop(left, c, q, left_send, left_recv, -1, part).wait_send()


def combine(sent, note, tiles, quarters):
    chunks, _, span, chunk = sent.shape
    width = chunks * chunk
    own = SR // quarters
    taps = halves_np(detect_taps(window_lags(), REACH))
    lag = np.arange(own + 2 * RIM)[None, :] - RIM - np.arange(own)[:, None]
    band = halves_np(detect_taps(lag, REACH))
    result = jax.ShapeDtypeStruct((own, width), F32)
    held = pltpu.VMEM((chunks, quarters, own, chunk), F32)
    every = pltpu.SemaphoreType.DMA((tiles * quarters,))
    pair = pltpu.SemaphoreType.DMA((chunks, tiles))
    step = pltpu.SemaphoreType.DMA((chunks, quarters))
    side = pltpu.SemaphoreType.DMA((chunks, 2))
    return pl.pallas_call(
        functools.partial(combine_body, tiles, quarters),
        out_shape=(result, result),
        in_specs=[pl.BlockSpec(memory_space=pltpu.VMEM)] * 4,
        out_specs=[pl.BlockSpec(memory_space=pltpu.VMEM)] * 2,
        scratch_shapes=[
            pltpu.VMEM(sent.shape, F32),
            pltpu.VMEM((quarters,) + note.shape, F32),
            pltpu.VMEM((SR, tiles * span), BF16),
            held,
            held,
            held,
            pltpu.VMEM((chunks, own + 2 * RIM, chunk), F32),
            pltpu.VMEM((own, LANES), F32),
            every, every, pair, pair, step, step, step, step, side, side,
        ],
        compiler_params=pltpu.CompilerParams(
            vmem_limit_bytes=52 * 2**20, collective_id=0, has_side_effects=True
        ),
        name="combine",
    )(note, sent, taps, band)


def shards(pieces, coeffs, weights, routes, offsets):
    tiles, quarters = lax.axis_size("tile"), lax.axis_size("vis")
    count, rows, width = pieces.shape
    capacity = max(2, 2 * count // tiles)
    sent, note = match(pieces, coeffs, weights, routes[:, 0], offsets, tiles, capacity)
    sent = sent.reshape(width // CHUNK, tiles, capacity * rows, CHUNK)
    return combine(sent, note, tiles, quarters)


def solution(mesh):
    placed = (
        P(("tile", "vis"), None, None),
        P(("tile", "vis"), None, None),
        P(("tile", "vis")),
        P(("tile", "vis"), None),
        P(("tile", "vis")),
    )
    return jax.shard_map(
        shards,
        mesh=mesh,
        in_specs=placed,
        out_specs=(P(("tile", "vis"), None), P(("tile", "vis"), None)),
        check_vma=False,
    )
```
